32 devices in a mesh: lat: 16 (over z, y, core), lon: 2 (over x).
Axes of the slice: x: 2, y: 2, z: 4, core: 2. Of those that a mesh axis runs over, the one named last changes fastest.
Arguments:
- source_field: bfloat16 [384, 768, 384], P('lat', 'lon'), may hold values from -6 to 6
- cotangent: bfloat16 [384, 768, 384], P('lat', 'lon'), may hold values from -6 to 6
- weight: bfloat16 [3, 384, 384], replicated, may hold values from -0.1875 to 0.1875
- spectral_gain: float32 [384, 384], replicated, may hold values from 0.1 to 1.9
- legendre: bfloat16 [384, 384, 384], P(('lat', 'lon')), may hold values from -0.3125 to 0.3125
- support_lat: int32 [384, 16], replicated, may hold values from -2 to 2
- support_lon: int32 [384, 16], replicated, may hold values from -4 to 4
- support_val: float32 [384, 16, 3], replicated, may hold values from -1.5 to 1.5
- order_map: int32 [384], replicated, may hold values from 0 to 383, each once
Outputs:
- result: bfloat16 [384, 768, 384], P('lat', 'lon')
- grad_input: bfloat16 [384, 768, 384], P('lat', 'lon')
- grad_weight: float32 [3, 384, 384], replicated
- grad_gain: float32 [384, 384], replicated
The draws below stay inside these ranges and needn't reach their ends.
Inputs may be any that keep to these rules, and one draw needn't show every extreme that they name: `order_map`: each order appears once.
All inputs are finite; a program needn't handle non-finite values.
Results may differ from the reference program's by a relative error of at most 0.009.
Values may be sent and summed in bfloat16 or wider, within the bound.
A program may use at most 512 MiB of HBM per device.

```python
import math
import jax
import jax.numpy as jnp
from jax import lax

C = 384
NLON = 768
M = 384
L = 384
K = 3
H = 2
DW = 4
S = 16
LAT_DEV = 24
NLAT = 384
N_LAT = 16


def set_ends(drawn, stream_key, smallest, high):
    index_at = [jax.random.randint(jax.random.fold_in(stream_key, axis), (), 0, length) for axis, length in enumerate(drawn.shape)]
    main_axis = drawn.shape.index(max(drawn.shape))
    beside = index_at[:main_axis] + [(index_at[main_axis] + 1) % drawn.shape[main_axis]] + index_at[main_axis + 1:]
    return drawn.at[tuple(index_at)].set(smallest).at[tuple(beside)].set(high)


def shard_levels(rng, extent, shards, low, top_value):
    def one(position, shards_of):
        steps = jax.random.uniform(jax.random.fold_in(jax.random.fold_in(rng, 6), position), (shards_of,), jnp.float32, low / len(shards), top_value / len(shards))
        return jnp.repeat(jnp.exp(steps), extent[position] // shards_of).reshape((-1,) + (1,) * (len(extent) - position - 1))

    factor_of = one(*shards[0])
    for cut in shards[1:]:
        factor_of = factor_of * one(*cut)
    return factor_of


def gaussian(key, dims, spread, limit, shards=(), kind=jnp.bfloat16):
    array = jax.random.normal(key, dims, jnp.float32) * spread
    if len(shards) > 0:
        array = shard_levels(key, dims, shards, -0.22, 0.18) * array
    return jnp.clip(array, min=-limit, max=limit).astype(kind)


def setup_inputs(seed: int = 0) -> dict:
    splits = jax.random.split(jax.random.key(seed), 10)
    return {
        "source_field": gaussian(splits[0], (NLAT, NLON, C), 1.0, 6.0, ((0, 16), (1, 2))),
        "cotangent": gaussian(splits[1], (NLAT, NLON, C), 1.0, 6.0, ((0, 16), (1, 2))),
        "weight": gaussian(splits[2], (K, C, C), (K * C) ** -0.5, 0.1875),
        "spectral_gain": jnp.clip(1.0 + 0.18 * jax.random.normal(splits[3], (L, C), jnp.float32), 0.1, 1.9),
        "legendre": gaussian(splits[4], (M, L, NLAT), NLAT ** -0.5, 0.3125, ((0, 32),)),
        "support_lat": set_ends(jax.random.randint(splits[5], (NLAT, S), 0 - H, H + 1), jax.random.fold_in(splits[5], 1), 0 - H, H).astype(jnp.int32),
        "support_lon": set_ends(jax.random.randint(splits[6], (NLAT, S), 0 - DW, DW + 1), jax.random.fold_in(splits[6], 1), 0 - DW, DW).astype(jnp.int32),
        "support_val": gaussian(splits[7], (NLAT, S, K), S ** -0.5, 1.5, (), jnp.float32),
        "order_map": jax.random.permutation(splits[8], M).astype(jnp.int32),
    }


SQRT_HALF = 0.7071067811865476
INV_SQRT_TAU = 0.3989422804014327

def gelu_value(values):
    return 0.5 * values * (1.0 + lax.erf(values * SQRT_HALF))

def gelu_slope(values):
    return 0.5 * (1.0 + lax.erf(values * SQRT_HALF)) + values * INV_SQRT_TAU * jnp.exp(-0.5 * values * values)

def tap_table(support_lat, support_lon, support_val):
    lat_steps = jnp.arange(2 * H + 1, dtype=jnp.int32) - H
    lon_steps = jnp.arange(2 * DW + 1, dtype=jnp.int32) - DW
    lat_onehot = (support_lat[:, :, None] == lat_steps[None, None, :]).astype(jnp.float32)
    lon_onehot = (support_lon[:, :, None] == lon_steps[None, None, :]).astype(jnp.float32)
    return jnp.einsum('tsk,tsa,tsd->tkad', support_val.astype(jnp.float32), lat_onehot, lon_onehot, precision=lax.Precision.HIGHEST)

def dft_table(order_map):
    frequency = jnp.repeat(order_map.astype(jnp.int32), 2)
    component = jnp.arange(frequency.shape[0], dtype=jnp.int32) % 2
    longitude = jnp.arange(NLON, dtype=jnp.int32)
    cycles = longitude[:, None] * frequency[None, :] % NLON
    angles = cycles.astype(jnp.float32) * (2.0 * math.pi / NLON)
    matrix = jnp.where(component[None, :] == 0, jnp.cos(angles), -jnp.sin(angles)) * math.sqrt(2.0 / NLON)
    return matrix.astype(jnp.bfloat16)

def apply_taps(padded, tap_rows, row_count, col_count, mirror):
    summed = jnp.zeros((row_count, col_count, K, padded.shape[2]), jnp.float32)
    for lat_tap in range(2 * H + 1):
        for lon_tap in range(2 * DW + 1):
            if mirror:
                row_start = 2 * H - lat_tap
                col_start = 2 * DW - lon_tap
                tap_coef = tap_rows[row_start:row_start + row_count, :, lat_tap, lon_tap]
            else:
                row_start = lat_tap
                col_start = lon_tap
                tap_coef = tap_rows[H:H + row_count, :, lat_tap, lon_tap]
            window = padded[row_start:row_start + row_count, col_start:col_start + col_count, :].astype(jnp.float32)
            summed = summed + tap_coef[:, None, :, None] * window[:, :, None, :]
    return summed.astype(jnp.bfloat16)

def wrap_pad(field):
    lon_padded = jnp.concatenate([field[:, NLON - DW:], field, field[:, :DW]], axis=1)
    return jnp.pad(lon_padded, ((H, H), (0, 0), (0, 0)))

def reference(source_field, cotangent, weight, spectral_gain, legendre, support_lat, support_lon, support_val, order_map):
    lat_total = LAT_DEV * N_LAT
    tap_weights = tap_table(support_lat, support_lon, support_val)
    tap_pad = jnp.pad(tap_weights, ((H, H), (0, 0), (0, 0), (0, 0)))
    dft_matrix = dft_table(order_map).astype(jnp.float32)
    quad_weights = jnp.sin(math.pi * (jnp.arange(lat_total, dtype=jnp.int32).astype(jnp.float32) + 0.5) / lat_total)
    flat_weight = weight.reshape(K * C, C)
    source_pad = wrap_pad(source_field)
    block_ids = jnp.arange(N_LAT, dtype=jnp.int32)

    def band_taps(block_number):
        offset = block_number * LAT_DEV
        window = lax.dynamic_slice_in_dim(source_pad, offset, LAT_DEV + 2 * H, 0)
        tap_rows = lax.dynamic_slice_in_dim(tap_pad, offset, LAT_DEV + 2 * H, 0)
        return apply_taps(window, tap_rows, LAT_DEV, NLON, False).reshape(LAT_DEV * NLON, K * C)

    def forward_band(block_number):
        offset = block_number * LAT_DEV
        conv_out = jnp.dot(band_taps(block_number), flat_weight, preferred_element_type=jnp.float32).astype(jnp.bfloat16)
        hidden = gelu_value(conv_out.astype(jnp.float32)).astype(jnp.bfloat16).reshape(LAT_DEV, NLON, C)
        band_quad = lax.dynamic_slice_in_dim(quad_weights, offset, LAT_DEV, 0)
        spectral = jnp.einsum('tpc,pj->tjc', hidden.astype(jnp.float32), dft_matrix) * band_quad[:, None, None]
        return (conv_out.reshape(LAT_DEV, NLON, C), spectral.astype(jnp.bfloat16))
    conv_out, spectral = lax.map(forward_band, block_ids)
    conv_out = conv_out.reshape(lat_total, NLON, C)
    spectral = spectral.reshape(lat_total, M, 2, C)
    table_wide = legendre.astype(jnp.float32)
    coefficients = jnp.einsum('olt,toqc->olqc', table_wide, spectral.astype(jnp.float32))
    filtered = (spectral_gain[None, :, None, :] * coefficients).astype(jnp.bfloat16)
    synthesized = jnp.einsum('olt,olqc->toqc', table_wide, filtered.astype(jnp.float32)).astype(jnp.bfloat16)
    synthesized = synthesized.reshape(N_LAT, LAT_DEV, 2 * M, C)
    conv_bands = conv_out.reshape(N_LAT, LAT_DEV, NLON, C)

    def output_band(pair):
        synth_band, conv_band = pair
        branch = jnp.einsum('tjc,pj->tpc', synth_band.astype(jnp.float32), dft_matrix).astype(jnp.bfloat16)
        return (conv_band.astype(jnp.float32) + branch.astype(jnp.float32)).astype(jnp.bfloat16)
    result = lax.map(output_band, (synthesized, conv_bands)).reshape(lat_total, NLON, C)

    def cot_band(cot_rows):
        return jnp.einsum('tpc,pj->tjc', cot_rows.astype(jnp.float32), dft_matrix).astype(jnp.bfloat16)
    cot_spectral = lax.map(cot_band, cotangent.reshape(N_LAT, LAT_DEV, NLON, C)).reshape(lat_total, M, 2, C)
    cot_coefficients = jnp.einsum('olt,toqc->olqc', table_wide, cot_spectral.astype(jnp.float32))
    grad_gain = lax.optimization_barrier(jnp.sum(coefficients * cot_coefficients, axis=(0, 2))) / math.sqrt(2.0 * M)
    cot_filtered = (spectral_gain[None, :, None, :] * cot_coefficients).astype(jnp.bfloat16)
    cot_synth = jnp.einsum('olt,olqc->toqc', table_wide, cot_filtered.astype(jnp.float32))
    cot_synth = (cot_synth * quad_weights[:, None, None, None]).astype(jnp.bfloat16)
    cot_synth = cot_synth.reshape(N_LAT, LAT_DEV, 2 * M, C)

    def cot_conv_band(triple):
        synth_band, conv_band, cot_rows = triple
        cot_hidden = jnp.einsum('tjc,pj->tpc', synth_band.astype(jnp.float32), dft_matrix).astype(jnp.bfloat16)
        slope = gelu_slope(conv_band.astype(jnp.float32))
        return (cot_rows.astype(jnp.float32) + cot_hidden.astype(jnp.float32) * slope).astype(jnp.bfloat16)
    cot_conv = lax.map(cot_conv_band, (cot_synth, conv_bands, cotangent.reshape(N_LAT, LAT_DEV, NLON, C)))
    cot_conv = cot_conv.reshape(lat_total, NLON, C)
    cot_pad = wrap_pad(cot_conv)

    def grad_band(summed, block_number):
        offset = block_number * LAT_DEV
        taps_flat = band_taps(block_number)
        cot_rows = lax.dynamic_slice_in_dim(cot_conv, offset, LAT_DEV, 0).reshape(LAT_DEV * NLON, C)
        partial_sum = jnp.dot(taps_flat.T, cot_rows, preferred_element_type=jnp.float32)
        window = lax.dynamic_slice_in_dim(cot_pad, offset, LAT_DEV + 2 * H, 0)
        tap_rows = lax.dynamic_slice_in_dim(tap_pad, offset, LAT_DEV + 2 * H, 0)
        back_taps = apply_taps(window, tap_rows, LAT_DEV, NLON, True).reshape(LAT_DEV * NLON, K, C)
        grad_rows = jnp.einsum('nkf,kcf->nc', back_taps.astype(jnp.float32), weight.astype(jnp.float32))
        return (summed + partial_sum, grad_rows.astype(jnp.bfloat16))
    summed, grad_input = lax.scan(grad_band, jnp.zeros((K * C, C), jnp.float32), block_ids)
    grad_input = grad_input.reshape(lat_total, NLON, C)
    grad_weight = (summed / math.sqrt(1.0 * lat_total * NLON)).reshape(K, C, C)
    return (result, grad_input, grad_weight, grad_gain)
```

```python
import math

import jax
import jax.numpy as jnp
from jax import lax
from jax.experimental import pallas as pl
from jax.experimental.pallas import tpu as pltpu
from jax.sharding import PartitionSpec as P

NLON = 768
M = 384
K = 3
H = 2
DW = 4


SQRT_HALF = 0.7071067811865476
INV_SQRT_TAU = 0.3989422804014327


def extended(block, sides, width, periodic):
    for axis, dim in sides:
        count = lax.axis_size(axis)
        forward = [(i, i + 1) for i in range(count - 1)]
        if periodic:
            forward.append((count - 1, 0))
        backward = [(target, source) for source, target in forward]
        low = lax.ppermute(
            lax.slice_in_dim(block, block.shape[dim] - width, None, axis=dim), axis, forward
        )
        high = lax.ppermute(lax.slice_in_dim(block, 0, width, axis=dim), axis, backward)
        block = jnp.concatenate([low, block, high], axis=dim)
    return block


def gelu_value(values):
    return 0.5 * values * (1.0 + lax.erf(values * SQRT_HALF))


def gelu_slope(values):
    return 0.5 * (1.0 + lax.erf(values * SQRT_HALF)) + values * INV_SQRT_TAU * jnp.exp(
        -0.5 * values * values
    )


def tap_table(support_lat, support_lon, support_val):
    lat_steps = jnp.arange(2 * H + 1, dtype=jnp.int32) - H
    lon_steps = jnp.arange(2 * DW + 1, dtype=jnp.int32) - DW
    lat_onehot = (support_lat[:, :, None] == lat_steps[None, None, :]).astype(jnp.float32)
    lon_onehot = (support_lon[:, :, None] == lon_steps[None, None, :]).astype(jnp.float32)
    return jnp.einsum(
        "tsk,tsa,tsd->tkad", support_val, lat_onehot, lon_onehot, precision=lax.Precision.HIGHEST
    )


def dft_table(order_map):
    frequency = jnp.repeat(order_map, 2)
    component = jnp.arange(frequency.shape[0], dtype=jnp.int32) % 2
    longitude = jnp.arange(NLON, dtype=jnp.int32)
    cycles = longitude[:, None] * frequency[None, :] % NLON
    angles = cycles.astype(jnp.float32) * (2.0 * math.pi / NLON)
    matrix = jnp.where(component[None, :] == 0, jnp.cos(angles), -jnp.sin(angles)) * math.sqrt(
        2.0 / NLON
    )
    return matrix.astype(jnp.bfloat16)


P_BLOCK = 96
Q_BLOCK = 128
N_LAT_TAPS = 2 * H + 1


def tap_coefficients(tap_rows, row_count, mirror):
    coef_list = []
    for place in range(N_LAT_TAPS):
        if mirror:
            taken = tap_rows[place : place + row_count, :, N_LAT_TAPS - 1 - place, ::-1]
        else:
            taken = tap_rows[H : H + row_count, :, place, :]
        coef_list.append(taken)
    coefs = jnp.stack(coef_list, axis=2).reshape(row_count, K * N_LAT_TAPS, 2 * DW + 1)
    return jnp.pad(coefs, ((0, 0), (0, 1), (0, Q_BLOCK - 2 * DW - 1)))


def fill_taps(coef_ref, window_refs, band_ref, taps_ref):
    for k in range(K):
        for place in range(N_LAT_TAPS):
            index = k * N_LAT_TAPS + place
            row = jnp.broadcast_to(coef_ref[0, index : index + 1, :], (P_BLOCK, Q_BLOCK))
            band = pltpu.roll(row, 0, 1, stride=1, stride_axis=0)
            band_ref[
                k * P_BLOCK : (k + 1) * P_BLOCK, place * Q_BLOCK : (place + 1) * Q_BLOCK
            ] = band.astype(jnp.bfloat16)
    col_count, wide = taps_ref.shape
    chan_count = wide // K
    for start in range(0, col_count, P_BLOCK):
        window = jnp.concatenate([ref[0, start : start + Q_BLOCK, :] for ref in window_refs], axis=0)
        summed = jnp.dot(band_ref[...], window, preferred_element_type=jnp.float32)
        for k in range(K):
            taps_ref[start : start + P_BLOCK, k * chan_count : (k + 1) * chan_count] = summed[
                k * P_BLOCK : (k + 1) * P_BLOCK
            ].astype(jnp.bfloat16)


def conv_kernel(coef_ref, w0, w1, w2, w3, w4, weight_ref, conv_ref, band_ref, taps_ref):
    fill_taps(coef_ref, (w0, w1, w2, w3, w4), band_ref, taps_ref)
    conv_ref[0] = jnp.dot(
        taps_ref[...], weight_ref[...], preferred_element_type=jnp.float32
    ).astype(jnp.bfloat16)


def back_kernel(
    coef_ref, w0, w1, w2, w3, w4, weight_ref, source_ref, input_ref, weight_grad_ref, band_ref, taps_ref
):
    fill_taps(coef_ref, (w0, w1, w2, w3, w4), band_ref, taps_ref)
    input_ref[0] = jnp.dot(
        taps_ref[...], weight_ref[...], preferred_element_type=jnp.float32
    ).astype(jnp.bfloat16)

    @pl.when(pl.program_id(0) == 0)
    def _():
        weight_grad_ref[...] = jnp.zeros_like(weight_grad_ref)

    weight_grad_ref[...] += lax.dot_general(
        source_ref[0], taps_ref[...], (((0,), (0,)), ((), ())), preferred_element_type=jnp.float32
    )


def tap_call(kernel, padded, coefs, flat_weight, col_count, source=None):
    row_count = coefs.shape[0]
    wide_count, chan_count = padded.shape[1:]

    def window_spec(place):
        return pl.BlockSpec((1, wide_count, chan_count), lambda t: (t + place, 0, 0))

    row_spec = pl.BlockSpec((1, col_count, chan_count), lambda t: (t, 0, 0))
    in_specs = [pl.BlockSpec((1,) + coefs.shape[1:], lambda t: (t, 0, 0))]
    in_specs += [window_spec(place) for place in range(N_LAT_TAPS)]
    in_specs += [pl.BlockSpec(flat_weight.shape, lambda t: (0, 0))]
    operands = [coefs] + [padded] * N_LAT_TAPS + [flat_weight]
    row_shape = jax.ShapeDtypeStruct((row_count, col_count, chan_count), jnp.bfloat16)
    positions = row_count * col_count
    flops = 2 * positions * chan_count * K * (N_LAT_TAPS * Q_BLOCK + chan_count)
    if source is None:
        out_specs, out_shape = row_spec, row_shape
    else:
        in_specs.append(row_spec)
        operands.append(source)
        grad_shape = (chan_count, K * chan_count)
        out_specs = (row_spec, pl.BlockSpec(grad_shape, lambda t: (0, 0)))
        out_shape = (row_shape, jax.ShapeDtypeStruct(grad_shape, jnp.float32))
        flops += 2 * positions * chan_count * K * chan_count
    return pl.pallas_call(
        kernel,
        grid=(row_count,),
        in_specs=in_specs,
        out_specs=out_specs,
        out_shape=out_shape,
        scratch_shapes=[
            pltpu.VMEM((K * P_BLOCK, N_LAT_TAPS * Q_BLOCK), jnp.bfloat16),
            pltpu.VMEM((col_count, K * chan_count), jnp.bfloat16),
        ],
        compiler_params=pltpu.CompilerParams(vmem_limit_bytes=48 * 1024 * 1024),
        cost_estimate=pl.CostEstimate(
            flops=flops, bytes_accessed=2 * 8 * positions * chan_count, transcendentals=0
        ),
    )(*operands)


def padded_field(field):
    lon_padded = extended(field, (("lon", 1),), DW, True)
    lon_padded = jnp.pad(lon_padded, ((0, 0), (0, Q_BLOCK - P_BLOCK - 2 * DW), (0, 0)))
    return extended(lon_padded, (("lat", 0),), H, False)


def to_lines(field):
    count = lax.axis_size("lon")
    parts = field.reshape((count, field.shape[0] // count) + field.shape[1:])
    return lax.all_to_all(parts, "lon", split_axis=0, concat_axis=0, tiled=True)


def to_grid(parts):
    moved = lax.all_to_all(parts, "lon", split_axis=0, concat_axis=0, tiled=True)
    return moved.reshape((-1,) + parts.shape[2:])


def to_spec(field):
    count = lax.axis_size("lat") * lax.axis_size("lon")
    rows, cols, chans = field.shape
    parts = field.reshape(rows, count, cols // count, chans).transpose(1, 0, 2, 3)
    moved = lax.all_to_all(parts, ("lat", "lon"), split_axis=0, concat_axis=0, tiled=True)
    return moved.reshape(count * rows, cols // count, chans)


def to_line_rows(field):
    count = lax.axis_size("lat") * lax.axis_size("lon")
    rows, cols, chans = field.shape
    parts = field.reshape(count, rows // count, cols, chans)
    moved = lax.all_to_all(parts, ("lat", "lon"), split_axis=0, concat_axis=0, tiled=True)
    return moved.transpose(1, 0, 2, 3).reshape(rows // count, count * cols, chans)


def legendre_in(spectral, table_rows):
    lat_total, col_total, chan_total = spectral.shape
    halves = spectral.reshape(lat_total, col_total // 2, 2, chan_total)
    return jnp.einsum("olt,toqc->olqc", table_rows, halves, preferred_element_type=jnp.float32)


def legendre_out(coefficients, table_rows):
    synthesis = jnp.einsum(
        "olt,olqc->toqc", table_rows, coefficients, preferred_element_type=jnp.float32
    )
    lat_total, order_count, two_parts, chan_total = synthesis.shape
    return synthesis.reshape(lat_total, order_count * two_parts, chan_total)


def body(
    source_field,
    cotangent,
    weight,
    spectral_gain,
    legendre,
    support_lat,
    support_lon,
    support_val,
    order_map,
):
    row_count, col_count, chan_count = source_field.shape
    lon_devices = lax.axis_size("lon")
    lat_total = row_count * lax.axis_size("lat")
    band_index = lax.axis_index("lat")
    block_index = lax.axis_index("lon")
    tap_weights = tap_table(support_lat, support_lon, support_val)
    tap_pad = jnp.pad(tap_weights, ((H, H), (0, 0), (0, 0), (0, 0)))
    tap_rows = lax.dynamic_slice_in_dim(tap_pad, band_index * row_count, row_count + 2 * H, 0)
    dft_matrix = dft_table(order_map)
    dft_parts = dft_matrix.reshape(lon_devices, col_count, dft_matrix.shape[1])
    flat_weight = weight.reshape(K * chan_count, chan_count)
    flat_weight_back = weight.transpose(0, 2, 1).reshape(K * chan_count, chan_count)
    all_rows = jnp.arange(lat_total, dtype=jnp.int32).astype(jnp.float32)
    quad_all = jnp.sin(math.pi * (all_rows + 0.5) / lat_total)
    line_rows = row_count // lon_devices
    line_quad = lax.dynamic_slice_in_dim(
        quad_all, band_index * row_count + block_index * line_rows, line_rows, 0
    )
    cot_line_spec = jnp.einsum(
        "nrpc,npj->rjc", to_lines(cotangent), dft_parts, preferred_element_type=jnp.float32
    )
    cot_spectral = to_spec(cot_line_spec.astype(jnp.bfloat16))
    conv_out = tap_call(
        conv_kernel,
        padded_field(source_field),
        tap_coefficients(tap_rows, row_count, False),
        flat_weight,
        col_count,
    )
    conv_wide = conv_out.astype(jnp.float32)
    hidden = gelu_value(conv_wide).astype(jnp.bfloat16)
    line_spec = jnp.einsum(
        "nrpc,npj->rjc", to_lines(hidden), dft_parts, preferred_element_type=jnp.float32
    )
    spectral = to_spec((line_spec * line_quad[:, None, None]).astype(jnp.bfloat16))
    cot_coefficients = legendre_in(cot_spectral, legendre)
    cot_filtered = (spectral_gain[None, :, None, :] * cot_coefficients).astype(jnp.bfloat16)
    cot_synth = legendre_out(cot_filtered, legendre)
    cot_synth = (cot_synth * quad_all[:, None, None]).astype(jnp.bfloat16)
    cot_synth_lines = to_line_rows(cot_synth)
    coefficients = legendre_in(spectral, legendre)
    gain_part = jnp.sum(coefficients * cot_coefficients, axis=(0, 2))
    filtered = (spectral_gain[None, :, None, :] * coefficients).astype(jnp.bfloat16)
    synth_lines = to_line_rows(legendre_out(filtered, legendre).astype(jnp.bfloat16))
    cot_hidden = jnp.einsum(
        "rjc,npj->nrpc", cot_synth_lines, dft_parts, preferred_element_type=jnp.float32
    ).astype(jnp.bfloat16)
    cot_hidden_grid = to_grid(cot_hidden)
    cot_conv = (
        cotangent.astype(jnp.float32) + cot_hidden_grid.astype(jnp.float32) * gelu_slope(conv_wide)
    ).astype(jnp.bfloat16)
    grad_input, weight_part = tap_call(
        back_kernel,
        padded_field(cot_conv),
        tap_coefficients(tap_rows, row_count, True),
        flat_weight_back,
        col_count,
        source_field,
    )
    branch = jnp.einsum(
        "rjc,npj->nrpc", synth_lines, dft_parts, preferred_element_type=jnp.float32
    ).astype(jnp.bfloat16)
    result = (conv_wide + to_grid(branch).astype(jnp.float32)).astype(jnp.bfloat16)
    weight_total = lax.psum(weight_part, ("lat", "lon")).reshape(chan_count, K, chan_count)
    gain_total = lax.psum(gain_part, ("lat", "lon"))
    grad_weight = weight_total.transpose(1, 0, 2) / math.sqrt(1.0 * lat_total * NLON)
    grad_gain = gain_total / math.sqrt(2.0 * M)
    return (result, grad_input, grad_weight, grad_gain)


def solution(mesh):
    return jax.shard_map(
        body,
        mesh=mesh,
        in_specs=(
            P("lat", "lon", None),
            P("lat", "lon", None),
            P(),
            P(),
            P(("lat", "lon"), None, None),
            P(),
            P(),
            P(),
            P(),
        ),
        out_specs=(P("lat", "lon", None), P("lat", "lon", None), P(), P()),
        check_vma=False,
    )
```
